32 devices in a mesh: parts: 2 (over y), pair: 4 (over z), aux: 2 (over x), occ: 2 (over core).
Axes of the slice: x: 2, y: 2, z: 4, core: 2. Of those that a mesh axis runs over, the one named last changes fastest.
Arguments:
- three_index: bfloat16 [64, 128, 16, 128], P(('parts', 'pair'), 'aux'), parts along dimension 0, may hold values from -0.5 to 0.5
- coefficients: bfloat16 [1024, 1024], P(('parts', 'pair'), 'occ'), parts along dimension 0, may hold values from -6 to 6
- shell_size: int32 [64], P(('parts', 'pair')), parts along dimension 0, may hold values from 1 to 10
- ket_shell: int32 [64, 8], P(('parts', 'pair')), parts along dimension 0, may hold values from 0 to 31
- ket_count: int32 [64], P(('parts', 'pair')), parts along dimension 0, may hold values from 1 to 8
Outputs:
- exchange_k: float32 [1024, 384], P(('parts', 'pair', 'aux', 'occ')), parts along dimension 0
The draws below stay inside these ranges and needn't reach their ends.
There are 2 independent parts, one for each index of `parts`. The reference program is written for one: setup_inputs(seed, part) draws one part's arguments, and reference() takes and returns one part's arrays. A program takes and returns all parts, laid end to end along the dimension named above; each array names one. Nothing has to cross between parts.
All inputs are finite; a program needn't handle non-finite values.
Results may differ from the reference program's by a relative error of at most 0.0003.
Values may be sent and summed in bfloat16 or wider, within the bound.
A program may use at most 64 MiB of HBM per device.

```python
import math
import jax
import jax.numpy as jnp
from jax import lax

SP = 16
NKET = 8
OCC = 1024
SH_DEV = 8
NSH = 32
NBAS = 512
FN_DEV = 128
NAUX = 128
N_PAIR = 4


def place_ends(array, rng, smallest, top_value):
    longest = array.shape.index(max(array.shape))
    spots = []
    for shift in (0, 1):
        where = [jax.random.randint(jax.random.fold_in(rng, axis), (), 0, length) for axis, length in enumerate(array.shape)]
        where[longest] = (where[longest] + shift) % array.shape[longest]
        spots.append(tuple(where))
    return array.at[spots[0]].set(smallest).at[spots[1]].set(top_value)


def steps_of(stream_key, dims, cuts, low, high):
    def one(axis_at, blocks):
        steps = jax.random.uniform(jax.random.fold_in(jax.random.fold_in(stream_key, 6), axis_at), (blocks,), jnp.float32, low / len(cuts), high / len(cuts))
        return jnp.repeat(jnp.exp(steps), dims[axis_at] // blocks).reshape((-1,) + (1,) * (len(dims) - axis_at - 1))

    loudness = one(*cuts[0])
    for cut in cuts[1:]:
        loudness = loudness * one(*cut)
    return loudness


def scatter_about(own_key, shape, spread, limit, cuts=(), kind=jnp.bfloat16):
    array = jax.random.normal(own_key, shape, jnp.float32) * spread
    if len(cuts) > 0:
        array = steps_of(own_key, shape, cuts, -0.22, 0.18) * array
    return jnp.clip(array, min=-limit, max=limit).astype(kind)


def setup_inputs(seed: int = 0, part: int = 0) -> dict:
    splits = jax.random.split(jax.random.key(seed), 6)
    part_keys = jax.random.split(jax.random.fold_in(splits[5], part), 6)
    three_index = scatter_about(part_keys[0], (NSH, NAUX, SP, NKET * SP), (NKET * SP) ** -0.5, 0.5, ((0, 4), (1, 2)))
    coefficients = scatter_about(part_keys[1], (NBAS, OCC), 1.0, 6.0, ((0, 4), (1, 2)))
    shell_size = place_ends(jax.random.randint(part_keys[2], (NSH,), 1, SP * 5 // 8 + 1), jax.random.fold_in(part_keys[2], 1), 1, (SP * 5 // 8 + 1) - 1).astype(jnp.int32)
    ket_shell = place_ends(jax.random.randint(part_keys[3], (NSH, NKET), 0, NSH), jax.random.fold_in(part_keys[3], 1), 0, NSH - 1).astype(jnp.int32)
    ket_count = place_ends(jax.random.randint(part_keys[4], (NSH,), 1, NKET + 1), jax.random.fold_in(part_keys[4], 1), 1, NKET).astype(jnp.int32)
    return dict(three_index=three_index, coefficients=coefficients, shell_size=shell_size, ket_shell=ket_shell, ket_count=ket_count)


def reference(three_index, coefficients, shell_size, ket_shell, ket_count):
    lanes = jnp.arange(SP, dtype=jnp.int32)
    shell_mask = lanes[None, :] < shell_size[:, None]
    row_mask = shell_mask.reshape(NBAS)
    coef_masked = jnp.where(row_mask[:, None], coefficients, jnp.zeros_like(coefficients))
    scale = 1.0 / math.sqrt(NAUX * OCC)
    slot_ids = jnp.arange(NKET, dtype=jnp.int32)

    def one_shell(packed):
        kets, count, block, mask = packed
        index = (kets[:, None] * SP + lanes[None, :]).reshape(NKET * SP).astype(jnp.int32)
        rows = coef_masked[index]
        live = jnp.repeat(slot_ids < count, SP)
        rows = jnp.where(live[:, None], rows, jnp.zeros_like(rows))
        product = jnp.dot(block.reshape(NAUX * SP, NKET * SP), rows, preferred_element_type=jnp.float32)
        product = product.reshape(NAUX, SP, OCC) * mask.astype(jnp.float32)[None, :, None]
        return product.astype(jnp.bfloat16)

    def one_owner(previous, owner):
        first = (owner * SH_DEV).astype(jnp.int32)
        kets = lax.dynamic_slice_in_dim(ket_shell, first, SH_DEV, 0)
        counts = lax.dynamic_slice_in_dim(ket_count, first, SH_DEV, 0)
        blocks = lax.dynamic_slice_in_dim(three_index, first, SH_DEV, 0)
        masks = lax.dynamic_slice_in_dim(shell_mask, first, SH_DEV, 0)
        half = lax.map(one_shell, (kets, counts, blocks, masks))
        flat = jnp.transpose(half, (0, 2, 1, 3)).reshape(FN_DEV, NAUX * OCC)
        own = jnp.dot(flat, flat.T, preferred_element_type=jnp.float32) * scale
        cross = jnp.dot(previous, flat.T, preferred_element_type=jnp.float32) * scale
        return (flat, (own, cross))
    start = jnp.zeros((FN_DEV, NAUX * OCC), jnp.bfloat16)
    last, (owns, crosses) = lax.scan(one_owner, start, jnp.arange(N_PAIR, dtype=jnp.int32))
    lefts = jnp.transpose(crosses, (0, 2, 1))
    rights = jnp.concatenate([crosses[1:], jnp.zeros((1, FN_DEV, FN_DEV), jnp.float32)], axis=0)
    tiles = jnp.concatenate([lefts, owns, rights], axis=2)
    return tiles.reshape(NBAS, 3 * FN_DEV)
```

```python
import functools
import math

import jax
import jax.numpy as jnp
from jax import lax
from jax.experimental import pallas as pl
from jax.experimental.pallas import tpu as pltpu
from jax.sharding import PartitionSpec as P

MESH = pl.DeviceIdType.MESH
NT = (((1,), (1,)), ((), ()))


def kernel(sizes, t_hbm, coef, size, ket, cnt, out, t_own, t_nb, coefs, pick, weights, half, half_nb, info,
           info_in, info_s, tiles, flips, red_same, red_cross, local_sem, coef_send, coef_fwd, coef_recv,
           info_send, info_recv, t_send, t_fwd, t_recv, same_send, same_recv, cross_send, cross_recv):
    n_pair, n_aux, n_occ, width, slots, chunks = sizes
    shells, rows, span = t_own.shape
    orbitals = coef.shape[1]
    functions = shells * width
    n_red = n_aux * n_occ
    share = shells // n_occ
    half_rows = rows // 2
    step = half_rows // chunks
    piece = functions // n_aux
    out_rows = functions // n_red
    nbas = n_pair * functions
    z = lax.axis_index("pair")
    x = lax.axis_index("aux")
    c = lax.axis_index("occ")
    mine = x * n_occ + c
    has_up = z + 1 < n_pair
    has_down = z > 0
    sides = ((has_up, 1), (has_down, -1))
    pending = []

    def when(cond, make, act):
        if cond is None:
            act(make())
        else:
            @pl.when(cond)
            def _():
                act(make())

    def begin(make, cond=None):
        when(cond, make, lambda d: d.start())
        pending.append((cond, make))

    def arrive(make, cond=None):
        when(cond, make, lambda d: d.wait_recv())

    def remote(src, dst, s_sem, r_sem, **where):
        return lambda: pltpu.make_async_remote_copy(
            src_ref=src(), dst_ref=dst(), send_sem=s_sem(), recv_sem=r_sem(),
            device_id={k: v() for k, v in where.items()}, device_id_type=MESH)

    local = pltpu.make_async_copy(t_hbm, t_own, local_sem.at[0])
    local.start()

    barrier = pltpu.get_barrier_semaphore()
    for delta in range(n_red):
        other = lax.rem(mine + delta, n_red)
        ox, oc = other // n_occ, lax.rem(other, n_occ)
        if delta > 0:
            pl.semaphore_signal(barrier, inc=1, device_id={"aux": ox, "occ": oc}, device_id_type=MESH)
        for has, way in sides:
            @pl.when(has)
            def _():
                pl.semaphore_signal(
                    barrier, inc=1, device_id={"pair": z + way, "aux": ox, "occ": oc}, device_id_type=MESH)

    first = pl.multiple_of(z * functions, functions)
    fun = lax.broadcasted_iota(jnp.int32, (width, orbitals), 0)
    for b in range(shells):
        block = coef[b * width:(b + 1) * width, :].astype(jnp.float32)
        block = jnp.where(fun < size[b], block, 0.0).astype(jnp.bfloat16)
        coefs[pl.ds(pl.multiple_of(first + b * width, width), width), :] = block

    row = lax.broadcasted_iota(jnp.int32, info.shape, 0)
    lane = lax.broadcasted_iota(jnp.int32, info.shape, 1)
    packed = jnp.zeros(info.shape, jnp.int32)
    for b in range(shells):
        line = jnp.where(lane == slots, cnt[b], jnp.where(lane == slots + 1, size[b], 0))
        for s in range(slots):
            line = jnp.where(lane == s, ket[b, s], line)
        packed = jnp.where(row == b, line, packed)
    info[...] = packed

    ups, downs = has_up.astype(jnp.int32), has_down.astype(jnp.int32)
    pl.semaphore_wait(barrier, n_red - 1 + n_red * (ups + downs))

    def part(owner, who):
        at = pl.multiple_of(owner * functions + who * piece, piece)
        return coefs.at[pl.ds(at, piece), :]

    def hop(owner, way, s):
        k = 0 if way > 0 else 1
        return remote(lambda: part(owner, x), lambda: part(owner, x), lambda: coef_send.at[k, s],
                      lambda: coef_recv.at[k, s, 0], pair=lambda: z + way)

    def across(owner, k, s, delta):
        return remote(lambda: part(owner, x), lambda: part(owner, x), lambda: coef_fwd.at[k, s, delta],
                      lambda: coef_recv.at[k, s, delta], aux=lambda: lax.rem(x + delta, n_aux))

    def across_in(owner, k, s, delta):
        who = lax.rem(x - delta + n_aux, n_aux)
        return remote(lambda: part(owner, who), lambda: part(owner, who), lambda: coef_fwd.at[k, s, delta],
                      lambda: coef_recv.at[k, s, delta], aux=lambda: lax.rem(x + delta, n_aux))

    def t_part(ref, lead, side, who, j):
        at = side * half_rows + j * step
        return ref.at[pl.ds(who * share, share), pl.ds(at, step), :]

    def t_hop(k, j):
        way = 1 if k == 0 else -1
        side = 1 if k == 0 else 0
        return remote(lambda: t_part(t_hbm, None, side, c, j), lambda: t_part(t_nb, None, side, c, j),
                      lambda: t_send.at[k, j], lambda: t_recv.at[side, j, 0], pair=lambda: z + way)

    def t_in(side, j):
        return remote(lambda: t_part(t_nb, None, side, c, j), lambda: t_part(t_nb, None, side, c, j),
                      lambda: t_send.at[side, j], lambda: t_recv.at[side, j, 0],
                      pair=lambda: z + (1 if side == 0 else -1))

    def t_across(side, j, delta, who):
        return remote(lambda: t_part(t_nb, None, side, who, j), lambda: t_part(t_nb, None, side, who, j),
                      lambda: t_fwd.at[side, j, delta], lambda: t_recv.at[side, j, delta],
                      occ=lambda: lax.rem(c + delta, n_occ))

    def t_forward(j):
        for side, (has, _) in enumerate(sides):
            arrive(t_in(side, j), has)
            for delta in range(1, n_occ):
                begin(t_across(side, j, delta, c), has)

    def t_ready(side, j, has):
        for delta in range(1, n_occ):
            arrive(t_across(side, j, delta, lax.rem(c - delta + n_occ, n_occ)), has)

    def info_hop(k):
        way = 1 if k == 0 else -1
        return remote(lambda: info, lambda: info_in.at[1 - k], lambda: info_send.at[k],
                      lambda: info_recv.at[1 - k], pair=lambda: z + way)

    def select(which, ket_at, cnt_at):
        col = lax.broadcasted_iota(jnp.int32, (width, nbas), 1) - lax.broadcasted_iota(jnp.int32, (width, nbas), 0)

        @pl.loop(0, shells)
        def _(b):
            for s in range(slots):
                at = pl.multiple_of(b * span + s * width, width)
                hit = jnp.logical_and(col == ket_at(b, s) * width, cnt_at(b) > s)
                pick[which, pl.ds(at, width), :] = jnp.where(hit, 1.0, 0.0).astype(jnp.bfloat16)

    def gather(which):
        block = 256

        @pl.loop(0, shells * span // block)
        def _(i):
            at = pl.ds(pl.multiple_of(i * block, block), block)
            weights[which, at, :] = jnp.dot(
                pick[which, at, :], coefs[...], preferred_element_type=jnp.float32).astype(jnp.bfloat16)

    def ket_rows(which, b):
        return weights[which, pl.ds(pl.multiple_of(b * span, span), span), :]

    for k, (has, way) in enumerate(sides):
        begin(hop(z, way, 0), has)
    for k, (has, way) in enumerate(sides):
        begin(info_hop(k), has)
    select(2, lambda b, s: ket[b, s], lambda b: cnt[b])
    for s in range(n_pair - 1):
        for k, (has, way) in enumerate(sides):
            owner = z - way * (s + 1)
            here = (owner >= 0) if way > 0 else (owner < n_pair)
            arrive(hop(owner, way, s), here)
            if s < n_pair - 2:
                begin(hop(owner, way, s + 1), jnp.logical_and(here, has))
            for delta in range(1, n_aux):
                begin(across(owner, k, s, delta), here)
        if s == 0:
            for j in range(chunks):
                for k, (has, way) in enumerate(sides):
                    begin(t_hop(k, j), has)
    for side, (has, way) in enumerate(sides):
        @pl.when(has)
        def _():
            info_hop(1 - side)().wait_recv()
            move = pltpu.make_async_copy(info_in.at[side], info_s.at[side], local_sem.at[1 + side])
            move.start()
            move.wait()
            select(side, lambda b, s: info_s[side, b, s], lambda b: info_s[side, b, slots])
    for s in range(n_pair - 1):
        for k, (has, way) in enumerate(sides):
            owner = z - way * (s + 1)
            here = (owner >= 0) if way > 0 else (owner < n_pair)
            for delta in range(1, n_aux):
                arrive(across_in(owner, k, s, delta), here)

    gather(2)
    local.wait()

    @pl.loop(0, shells)
    def _(b):
        w = ket_rows(2, b)

        @pl.loop(0, 2)
        def _(r):
            at = pl.multiple_of(r * half_rows, half_rows)
            half[b, pl.ds(at, half_rows), :] = jnp.dot(
                t_own[b, pl.ds(at, half_rows), :], w, preferred_element_type=jnp.float32).astype(jnp.bfloat16)

    tiles[...] = jnp.zeros_like(tiles)
    unroll = 4

    def pages(ref, at):
        return ref[:, pl.ds(pl.multiple_of(at, width), width), :].reshape(functions, orbitals)

    def own_part(lo, hi):
        def body(i, acc):
            for u in range(unroll):
                a = pages(half, (lo + i * unroll + u) * width)
                acc = acc + lax.dot_general(a, a, NT, preferred_element_type=jnp.float32)
            return acc
        zero = jnp.zeros((functions, functions), jnp.float32)
        tiles[:, functions:2 * functions] += lax.fori_loop(0, (hi - lo) // unroll, body, zero)

    n_aux_rows = rows // width
    t_forward(0)
    own_part(0, n_aux_rows // 2)
    for side, (has, way) in enumerate(sides):
        @pl.when(has)
        def _():
            gather(side)
    if chunks > 1:
        t_forward(1)
    own_part(n_aux_rows // 2, n_aux_rows)
    for j in range(chunks):
        for side, (has, way) in enumerate(sides):
            t_ready(side, j, has)

            @pl.when(has)
            def _():
                at = side * half_rows + j * step

                @pl.loop(0, shells)
                def _(b):
                    half_nb[b] = jnp.dot(t_nb[b, at:at + step, :], ket_rows(side, b),
                                         preferred_element_type=jnp.float32).astype(jnp.bfloat16)

                def body(i, acc):
                    for u in range(unroll):
                        p = i * unroll + u
                        a = pages(half, at + p * width)
                        acc = acc + lax.dot_general(a, pages(half_nb, p * width), NT,
                                                    preferred_element_type=jnp.float32)
                    return acc
                zero = jnp.zeros((functions, functions), jnp.float32)
                col = 2 * functions if side == 0 else 0
                tiles[:, col:col + functions] += lax.fori_loop(0, step // width // unroll, body, zero)
        if j + 2 < chunks:
            t_forward(j + 2)
    flips[0] = tiles[:, 2 * functions:].T
    flips[1] = tiles[:, :functions].T

    def cut(ref, r):
        return ref.at[pl.ds(pl.multiple_of(r * out_rows, out_rows), out_rows), :]

    def same(delta):
        other = lax.rem(mine + delta, n_red)
        return remote(lambda: cut(tiles, other), lambda: red_same.at[delta], lambda: same_send.at[delta],
                      lambda: same_recv.at[delta], aux=lambda: other // n_occ, occ=lambda: lax.rem(other, n_occ))

    def cross(side, delta):
        other = lax.rem(mine + delta, n_red)
        way = 1 if side == 0 else -1
        return remote(lambda: cut(flips.at[side], other), lambda: red_cross.at[side, delta],
                      lambda: cross_send.at[side, delta], lambda: cross_recv.at[side, delta],
                      pair=lambda: z + way, aux=lambda: other // n_occ, occ=lambda: lax.rem(other, n_occ))

    for delta in range(n_red):
        for side, (has, way) in enumerate(sides):
            begin(cross(side, delta), has)
    for delta in range(1, n_red):
        begin(same(delta))

    total = tiles[pl.ds(pl.multiple_of(mine * out_rows, out_rows), out_rows), :]
    for delta in range(1, n_red):
        arrive(same(delta))
        total = total + red_same[delta]
    tiles_out = [total[:, i * functions:(i + 1) * functions] for i in range(3)]
    for side, (has, way) in enumerate(sides):
        comes = has_down if side == 0 else has_up
        for delta in range(n_red):
            arrive(cross(side, delta), comes)
        col = 0 if side == 0 else 2
        more = red_cross[side, 0]
        for delta in range(1, n_red):
            more = more + red_cross[side, delta]
        tiles_out[col] = jnp.where(comes, tiles_out[col] + more, 0.0)

    scale = 1.0 / math.sqrt(n_aux_rows * n_aux * orbitals * n_occ)
    r_id = lax.broadcasted_iota(jnp.int32, (out_rows, functions), 0) + mine * out_rows
    c_id = lax.broadcasted_iota(jnp.int32, (out_rows, functions), 1)
    r_size = jnp.zeros_like(r_id)
    for b in range(shells):
        r_size = jnp.where(r_id // width == b, size[b], r_size)
    r_live = lax.rem(r_id, width) < r_size
    for i in range(3):
        c_size = jnp.zeros_like(c_id)
        for b in range(shells):
            there = size[b] if i == 1 else info_s[1 if i == 0 else 0, b, slots + 1]
            c_size = jnp.where(c_id // width == b, there, c_size)
        live = jnp.logical_and(r_live, lax.rem(c_id, width) < c_size)
        out[:, i * functions:(i + 1) * functions] = jnp.where(live, tiles_out[i] * scale, 0.0)

    for cond, make in pending:
        when(cond, make, lambda d: d.wait_send())


def shards(chunks, three_index, coefficients, shell_size, ket_shell, ket_count):
    shells, aux_rows, width, span = three_index.shape
    slots = span // width
    n_pair, n_aux, n_occ = (lax.axis_size(a) for a in ("pair", "aux", "occ"))
    n_red = n_aux * n_occ
    orbitals = coefficients.shape[1]
    functions = shells * width
    rows = aux_rows * width
    out_rows = functions // n_red
    step = rows // 2 // chunks
    bf16, f32 = jnp.bfloat16, jnp.float32
    dma = pltpu.SemaphoreType.DMA
    smem = pl.BlockSpec(memory_space=pltpu.SMEM)
    vmem = pl.BlockSpec(memory_space=pltpu.VMEM)
    return pl.pallas_call(
        functools.partial(kernel, (n_pair, n_aux, n_occ, width, slots, chunks)),
        out_shape=jax.ShapeDtypeStruct((out_rows, 3 * functions), f32),
        in_specs=[pl.BlockSpec(memory_space=pl.ANY), vmem, smem, smem, smem],
        out_specs=vmem,
        scratch_shapes=[
            pltpu.VMEM((shells, rows, span), bf16),
            pltpu.VMEM((shells, rows, span), bf16),
            pltpu.VMEM((n_pair * functions, orbitals), bf16),
            pltpu.VMEM((3, shells * span, n_pair * functions), bf16),
            pltpu.VMEM((3, shells * span, orbitals), bf16),
            pltpu.VMEM((shells, rows, orbitals), bf16),
            pltpu.VMEM((shells, step, orbitals), bf16),
            pltpu.VMEM((shells, 128), jnp.int32),
            pltpu.VMEM((2, shells, 128), jnp.int32),
            pltpu.SMEM((2, shells, 128), jnp.int32),
            pltpu.VMEM((functions, 3 * functions), f32),
            pltpu.VMEM((2, functions, functions), f32),
            pltpu.VMEM((n_red, out_rows, 3 * functions), f32),
            pltpu.VMEM((2, n_red, out_rows, functions), f32),
            dma((3,)),
            dma((2, n_pair)),
            dma((2, n_pair, n_aux)),
            dma((2, n_pair, n_aux)),
            dma((2,)),
            dma((2,)),
            dma((2, chunks)),
            dma((2, chunks, n_occ)),
            dma((2, chunks, n_occ)),
            dma((n_red,)),
            dma((n_red,)),
            dma((2, n_red)),
            dma((2, n_red)),
        ],
        compiler_params=pltpu.CompilerParams(
            collective_id=0, has_side_effects=True, vmem_limit_bytes=48 * 1024 * 1024),
    )(three_index.reshape(shells, rows, span), coefficients, shell_size, ket_shell, ket_count)


def solution(mesh):
    return jax.shard_map(
        functools.partial(shards, 4),
        mesh=mesh,
        in_specs=(
            P(("parts", "pair"), "aux", None, None),
            P(("parts", "pair"), "occ"),
            P(("parts", "pair")),
            P(("parts", "pair"), None),
            P(("parts", "pair")),
        ),
        out_specs=P(("parts", "pair", "aux", "occ"), None),
        check_vma=False,
    )
```

```python
import functools
import math

import jax
import jax.numpy as jnp
from jax import lax
from jax.experimental import pallas as pl
from jax.experimental.pallas import tpu as pltpu
from jax.sharding import PartitionSpec as P

MESH = pl.DeviceIdType.MESH
NT = (((1,), (1,)), ((), ()))


def kernel(sizes, t_hbm, coef_hbm, size_hbm, ket_hbm, cnt_hbm, out, coef, size, ket, cnt, t_own, t_nb, coefs, pick, density, weights, left, spread, spread_nb, info,
           info_in, info_s, tiles, flips, red_same, red_cross, local_sem, coef_send, coef_recv, coef_fwd, coef_cross,
           info_send, info_recv, t_send, t_recv, same_send, same_recv, cross_send, cross_recv):
    n_pair, n_aux, n_occ, width, slots, chunks = sizes
    shells, rows, span = t_own.shape
    orbitals = coef.shape[1]
    functions = shells * width
    n_red = n_aux * n_occ
    half_rows = rows // 2
    step = half_rows // chunks
    out_rows = functions // n_red
    top = width * 5 // 8
    kept = shells * top
    nbas = coefs.shape[0]
    z = lax.axis_index("pair")
    x = lax.axis_index("aux")
    c = lax.axis_index("occ")
    mine = x * n_occ + c
    base = pl.multiple_of(c * rows, rows)
    has_up = z + 1 < n_pair
    has_down = z > 0
    sides = ((has_up, 1), (has_down, -1))
    pending = []

    def when(cond, make, act):
        if cond is None:
            act(make())
        else:
            @pl.when(cond)
            def _():
                act(make())

    def begin(make, cond=None):
        when(cond, make, lambda d: d.start())
        pending.append((cond, make))

    def arrive(make, cond=None):
        when(cond, make, lambda d: d.wait_recv())

    def remote(src, dst, s_sem, r_sem, **where):
        return lambda: pltpu.make_async_remote_copy(
            src_ref=src(), dst_ref=dst(), send_sem=s_sem(), recv_sem=r_sem(),
            device_id={k: v() for k, v in where.items()}, device_id_type=MESH)

    local = pltpu.make_async_copy(t_hbm.at[:, pl.ds(base, rows), :], t_own, local_sem.at[0])
    small = [pltpu.make_async_copy(src, dst, local_sem.at[3 + i]) for i, (src, dst) in enumerate(
        ((size_hbm, size), (coef_hbm, coef), (ket_hbm, ket), (cnt_hbm, cnt)))]
    for move in small:
        move.start()
    local.start()

    barrier = pltpu.get_barrier_semaphore()
    for delta in range(n_red):
        other = lax.rem(mine + delta, n_red)
        ox, oc = other // n_occ, lax.rem(other, n_occ)
        if delta > 0:
            pl.semaphore_signal(barrier, inc=1, device_id={"aux": ox, "occ": oc}, device_id_type=MESH)
        for has, way in sides:
            @pl.when(has)
            def _():
                pl.semaphore_signal(
                    barrier, inc=1, device_id={"pair": z + way, "aux": ox, "occ": oc}, device_id_type=MESH)

    for move in small:
        move.wait()
    fun = lax.broadcasted_iota(jnp.int32, (width, orbitals), 0)
    masked = jnp.concatenate([
        jnp.where(fun < size[b], coef[b * width:(b + 1) * width, :].astype(jnp.float32), 0.0)
        for b in range(shells)], axis=0).astype(jnp.bfloat16)
    to = lax.broadcasted_iota(jnp.int32, (kept, functions), 0)
    frm = lax.broadcasted_iota(jnp.int32, (kept, functions), 1)
    g = lax.rem(frm, width)
    packing = jnp.logical_and(to == (frm // width) * top + g, g < top)
    packing = jnp.where(packing, 1.0, 0.0).astype(jnp.bfloat16)
    mine_cols = pl.ds(pl.multiple_of(c * orbitals, orbitals), orbitals)
    coefs[pl.ds(pl.multiple_of(z * kept, kept), kept), mine_cols] = jnp.dot(
        packing, masked, preferred_element_type=jnp.float32).astype(jnp.bfloat16)
    if nbas > n_pair * kept:
        coefs[n_pair * kept:, :] = jnp.zeros((nbas - n_pair * kept, n_occ * orbitals), jnp.bfloat16)

    row = lax.broadcasted_iota(jnp.int32, info.shape, 0)
    lane = lax.broadcasted_iota(jnp.int32, info.shape, 1)
    packed = jnp.zeros(info.shape, jnp.int32)
    for b in range(shells):
        line = jnp.where(lane == slots, cnt[b], jnp.where(lane == slots + 1, size[b], 0))
        for s in range(slots):
            line = jnp.where(lane == s, ket[b, s], line)
        packed = jnp.where(row == b, line, packed)
    info[...] = packed

    ups, downs = has_up.astype(jnp.int32), has_down.astype(jnp.int32)
    pl.semaphore_wait(barrier, n_red - 1 + n_red * (ups + downs))

    def part(owner, who):
        return coefs.at[pl.ds(pl.multiple_of(owner * kept, kept), kept),
                        pl.ds(pl.multiple_of(who * orbitals, orbitals), orbitals)]

    def hop(owner, way, s):
        k = 0 if way > 0 else 1
        return remote(lambda: part(owner, c), lambda: part(owner, c), lambda: coef_send.at[k, s],
                      lambda: coef_recv.at[k, s], pair=lambda: z + way)

    def across(owner, k, s, delta, who):
        return remote(lambda: part(owner, who), lambda: part(owner, who), lambda: coef_fwd.at[k, s, delta],
                      lambda: coef_cross.at[k, s, delta], occ=lambda: lax.rem(c + delta, n_occ))

    def across_in(owner, k, s, delta):
        return across(owner, k, s, delta, lax.rem(c - delta + n_occ, n_occ))

    def t_hop(k, j):
        way, side = (1, 1) if k == 0 else (-1, 0)
        at = side * half_rows + j * step
        return remote(lambda: t_hbm.at[:, pl.ds(base + at, step), :], lambda: t_nb.at[:, pl.ds(at, step), :],
                      lambda: t_send.at[k, j], lambda: t_recv.at[side, j], pair=lambda: z + way)

    def info_hop(k):
        way = 1 if k == 0 else -1
        return remote(lambda: info, lambda: info_in.at[1 - k], lambda: info_send.at[k],
                      lambda: info_recv.at[1 - k], pair=lambda: z + way)

    def select(which, ket_at, cnt_at):
        col = lax.broadcasted_iota(jnp.int32, (width, nbas), 1) - lax.broadcasted_iota(jnp.int32, (width, nbas), 0)
        live = lax.broadcasted_iota(jnp.int32, (width, nbas), 0) < top

        @pl.loop(0, shells)
        def _(b):
            for s in range(slots):
                at = pl.multiple_of(b * span + s * width, width)
                hit = jnp.logical_and(jnp.logical_and(col == ket_at(b, s) * top, live), cnt_at(b) > s)
                pick[which, pl.ds(at, width), :] = jnp.where(hit, 1.0, 0.0).astype(jnp.bfloat16)

    def picked(which, b):
        return pick[which, pl.ds(pl.multiple_of(b * span, span), span), :]

    def scatter(which, lo, hi):
        @pl.loop(lo, hi)
        def _(b):
            spread[b] = jnp.dot(t_own[b], picked(which, b), preferred_element_type=jnp.float32).astype(jnp.bfloat16)

    for k, (has, way) in enumerate(sides):
        begin(hop(z, way, 0), has)
    for delta in range(1, n_occ):
        begin(across(z, 0, n_pair - 1, delta, c))
    for k, (has, way) in enumerate(sides):
        begin(info_hop(k), has)
    select(2, lambda b, s: ket[b, s], lambda b: cnt[b])
    local.wait()
    for s in range(n_pair - 1):
        for k, (has, way) in enumerate(sides):
            owner = z - way * (s + 1)
            here = (owner >= 0) if way > 0 else (owner < n_pair)
            arrive(hop(owner, way, s), here)
            if s < n_pair - 2:
                begin(hop(owner, way, s + 1), jnp.logical_and(here, has))
            for delta in range(1, n_occ):
                begin(across(owner, k, s, delta, c), here)
        if s == 0:
            for j in range(chunks):
                for k, (has, way) in enumerate(sides):
                    begin(t_hop(k, j), has)
            scatter(2, 0, shells // 2)
        if s == 1 or n_pair == 2:
            scatter(2, shells // 2, shells)
    for delta in range(1, n_occ):
        arrive(across_in(z, 0, n_pair - 1, delta))
    for s in range(n_pair - 1):
        for k, (has, way) in enumerate(sides):
            owner = z - way * (s + 1)
            here = (owner >= 0) if way > 0 else (owner < n_pair)
            for delta in range(1, n_occ):
                arrive(across_in(owner, k, s, delta), here)

    lines = 128

    @pl.loop(0, nbas // lines)
    def _(i):
        at = pl.ds(pl.multiple_of(i * lines, lines), lines)
        d = lax.dot_general(coefs[at, :], coefs[...], NT, preferred_element_type=jnp.float32)
        high = d.astype(jnp.bfloat16)
        density[0, at, :] = high
        density[1, at, :] = (d - high.astype(jnp.float32)).astype(jnp.bfloat16)

    for part_id in range(2):
        @pl.loop(0, shells)
        def _(b):
            weights[b, part_id * span:(part_id + 1) * span, :] = jnp.dot(
                picked(2, b), density[part_id], preferred_element_type=jnp.float32).astype(jnp.bfloat16)

    @pl.loop(0, shells)
    def _(b):
        t = t_own[b]
        left[b] = jnp.dot(jnp.concatenate([t, t], axis=1), weights[b],
                          preferred_element_type=jnp.float32).astype(jnp.bfloat16)

    tiles[...] = jnp.zeros_like(tiles)
    unroll = 4

    def pages(ref, at):
        return ref[:, pl.ds(pl.multiple_of(at, width), width), :].reshape(functions, nbas)

    def contract(other, at, count, off, col):
        def body(i, acc):
            for u in range(unroll):
                p = (i * unroll + u) * width
                acc = acc + lax.dot_general(pages(left, at + p), pages(other, p + off), NT,
                                            preferred_element_type=jnp.float32)
            return acc
        zero = jnp.zeros((functions, functions), jnp.float32)
        tiles[:, col:col + functions] += lax.fori_loop(0, count // width // unroll, body, zero)

    contract(spread, 0, rows, 0, functions)
    for side, (has, way) in enumerate(sides):
        @pl.when(has)
        def _():
            info_hop(1 - side)().wait_recv()
            move = pltpu.make_async_copy(info_in.at[side], info_s.at[side], local_sem.at[1 + side])
            move.start()
            move.wait()
            select(side, lambda b, s: info_s[side, b, s], lambda b: info_s[side, b, slots])
    for j in range(chunks):
        for side, (has, way) in enumerate(sides):
            @pl.when(has)
            def _():
                t_hop(1 - side, j)().wait_recv()
                at = side * half_rows + j * step

                @pl.loop(0, shells)
                def _(b):
                    spread_nb[b] = jnp.dot(t_nb[b, at:at + step, :], picked(side, b),
                                           preferred_element_type=jnp.float32).astype(jnp.bfloat16)
                contract(spread_nb, at, step, 0, 2 * functions if side == 0 else 0)
    flips[0] = tiles[:, 2 * functions:].T
    flips[1] = tiles[:, :functions].T

    def cut(ref, r):
        return ref.at[pl.ds(pl.multiple_of(r * out_rows, out_rows), out_rows), :]

    def same(delta):
        other = lax.rem(mine + delta, n_red)
        return remote(lambda: cut(tiles, other), lambda: red_same.at[delta], lambda: same_send.at[delta],
                      lambda: same_recv.at[delta], aux=lambda: other // n_occ, occ=lambda: lax.rem(other, n_occ))

    def cross(side, delta):
        other = lax.rem(mine + delta, n_red)
        way = 1 if side == 0 else -1
        return remote(lambda: cut(flips.at[side], other), lambda: red_cross.at[side, delta],
                      lambda: cross_send.at[side, delta], lambda: cross_recv.at[side, delta],
                      pair=lambda: z + way, aux=lambda: other // n_occ, occ=lambda: lax.rem(other, n_occ))

    for delta in range(n_red):
        for side, (has, way) in enumerate(sides):
            begin(cross(side, delta), has)
    for delta in range(1, n_red):
        begin(same(delta))

    total = tiles[pl.ds(pl.multiple_of(mine * out_rows, out_rows), out_rows), :]
    for delta in range(1, n_red):
        arrive(same(delta))
        total = total + red_same[delta]
    tiles_out = [total[:, i * functions:(i + 1) * functions] for i in range(3)]
    for side, (has, way) in enumerate(sides):
        comes = has_down if side == 0 else has_up
        for delta in range(n_red):
            arrive(cross(side, delta), comes)
        col = 0 if side == 0 else 2
        more = red_cross[side, 0]
        for delta in range(1, n_red):
            more = more + red_cross[side, delta]
        tiles_out[col] = jnp.where(comes, tiles_out[col] + more, 0.0)

    scale = 1.0 / math.sqrt(rows // width * n_red * orbitals * n_occ)
    r_id = lax.broadcasted_iota(jnp.int32, (out_rows, functions), 0) + mine * out_rows
    c_id = lax.broadcasted_iota(jnp.int32, (out_rows, functions), 1)
    r_size = jnp.zeros_like(r_id)
    for b in range(shells):
        r_size = jnp.where(r_id // width == b, size[b], r_size)
    r_live = lax.rem(r_id, width) < r_size
    for i in range(3):
        c_size = jnp.zeros_like(c_id)
        for b in range(shells):
            there = size[b] if i == 1 else info_s[1 if i == 0 else 0, b, slots + 1]
            c_size = jnp.where(c_id // width == b, there, c_size)
        live = jnp.logical_and(r_live, lax.rem(c_id, width) < c_size)
        out[:, i * functions:(i + 1) * functions] = jnp.where(live, tiles_out[i] * scale, 0.0)

    for cond, make in pending:
        when(cond, make, lambda d: d.wait_send())


def shards(chunks, three_index, coefficients, shell_size, ket_shell, ket_count):
    shells, aux_rows, width, span = three_index.shape
    slots = span // width
    n_pair, n_aux, n_occ = (lax.axis_size(a) for a in ("pair", "aux", "occ"))
    n_red = n_aux * n_occ
    orbitals = coefficients.shape[1]
    functions = shells * width
    rows = aux_rows * width // n_occ
    kept = n_pair * shells * (width * 5 // 8)
    nbas = -(-kept // 128) * 128
    out_rows = functions // n_red
    step = rows // 2 // chunks
    bf16, f32 = jnp.bfloat16, jnp.float32
    dma = pltpu.SemaphoreType.DMA
    vmem = pl.BlockSpec(memory_space=pltpu.VMEM)
    return pl.pallas_call(
        functools.partial(kernel, (n_pair, n_aux, n_occ, width, slots, chunks)),
        out_shape=jax.ShapeDtypeStruct((out_rows, 3 * functions), f32),
        in_specs=[pl.BlockSpec(memory_space=pl.ANY)] * 5,
        out_specs=vmem,
        scratch_shapes=[
            pltpu.VMEM((functions, orbitals), bf16),
            pltpu.SMEM((shells,), jnp.int32),
            pltpu.SMEM((shells, slots), jnp.int32),
            pltpu.SMEM((shells,), jnp.int32),
            pltpu.VMEM((shells, rows, span), bf16),
            pltpu.VMEM((shells, rows, span), bf16),
            pltpu.VMEM((nbas, n_occ * orbitals), bf16),
            pltpu.VMEM((3, shells * span, nbas), bf16),
            pltpu.VMEM((2, nbas, nbas), bf16),
            pltpu.VMEM((shells, 2 * span, nbas), bf16),
            pltpu.VMEM((shells, rows, nbas), bf16),
            pltpu.VMEM((shells, rows, nbas), bf16),
            pltpu.VMEM((shells, step, nbas), bf16),
            pltpu.VMEM((shells, 128), jnp.int32),
            pltpu.VMEM((2, shells, 128), jnp.int32),
            pltpu.SMEM((2, shells, 128), jnp.int32),
            pltpu.VMEM((functions, 3 * functions), f32),
            pltpu.VMEM((2, functions, functions), f32),
            pltpu.VMEM((n_red, out_rows, 3 * functions), f32),
            pltpu.VMEM((2, n_red, out_rows, functions), f32),
            dma((7,)),
            dma((2, n_pair)),
            dma((2, n_pair)),
            dma((2, n_pair, n_occ)),
            dma((2, n_pair, n_occ)),
            dma((2,)),
            dma((2,)),
            dma((2, chunks)),
            dma((2, chunks)),
            dma((n_red,)),
            dma((n_red,)),
            dma((2, n_red)),
            dma((2, n_red)),
        ],
        compiler_params=pltpu.CompilerParams(
            collective_id=0, has_side_effects=True, vmem_limit_bytes=64 * 1024 * 1024),
    )(three_index.reshape(shells, aux_rows * width, span), coefficients, shell_size, ket_shell, ket_count)


def solution(mesh):
    return jax.shard_map(
        functools.partial(shards, 2),
        mesh=mesh,
        in_specs=(
            P(("parts", "pair"), "aux", None, None),
            P(("parts", "pair"), "occ"),
            P(("parts", "pair")),
            P(("parts", "pair"), None),
            P(("parts", "pair")),
        ),
        out_specs=P(("parts", "pair", "aux", "occ"), None),
        check_vma=False,
    )
```

```python
import functools
import math

import jax
import jax.numpy as jnp
from jax import lax
from jax.experimental import pallas as pl
from jax.experimental.pallas import tpu as pltpu
from jax.sharding import PartitionSpec as P

MESH = pl.DeviceIdType.MESH
NT = (((1,), (1,)), ((), ()))


def kernel(sizes, t_hbm, coef_hbm, size_hbm, ket_hbm, cnt_hbm, out, coef, size, ket, cnt, t_own, t_nb, coefs, pick, narrow, widen, t_pack, density, weights, left, spread, spread_nb, info,
           info_in, info_s, tiles, flips, red_same, red_cross, local_sem, coef_send, coef_recv, coef_fwd, coef_cross,
           info_send, info_recv, t_send, t_recv, same_send, same_recv, cross_send, cross_recv):
    n_pair, n_aux, n_occ, width, slots, chunks = sizes
    shells, rows, span = t_own.shape
    orbitals = coef.shape[1]
    functions = shells * width
    n_red = n_aux * n_occ
    half_rows = rows // 2
    step = half_rows // chunks
    out_rows = functions // n_red
    top = width * 5 // 8
    kept = shells * top
    nbas = coefs.shape[0]
    z = lax.axis_index("pair")
    x = lax.axis_index("aux")
    c = lax.axis_index("occ")
    mine = x * n_occ + c
    base = pl.multiple_of(c * rows, rows)
    has_up = z + 1 < n_pair
    has_down = z > 0
    sides = ((has_up, 1), (has_down, -1))
    pending = []

    def when(cond, make, act):
        if cond is None:
            act(make())
        else:
            @pl.when(cond)
            def _():
                act(make())

    def begin(make, cond=None):
        when(cond, make, lambda d: d.start())
        pending.append((cond, make))

    def arrive(make, cond=None):
        when(cond, make, lambda d: d.wait_recv())

    def remote(src, dst, s_sem, r_sem, **where):
        return lambda: pltpu.make_async_remote_copy(
            src_ref=src(), dst_ref=dst(), send_sem=s_sem(), recv_sem=r_sem(),
            device_id={k: v() for k, v in where.items()}, device_id_type=MESH)

    local = pltpu.make_async_copy(t_hbm.at[:, pl.ds(base, rows), :], t_own, local_sem.at[0])
    small = [pltpu.make_async_copy(src, dst, local_sem.at[3 + i]) for i, (src, dst) in enumerate(
        ((size_hbm, size), (coef_hbm, coef), (ket_hbm, ket), (cnt_hbm, cnt)))]
    for move in small:
        move.start()
    local.start()

    barrier = pltpu.get_barrier_semaphore()
    for delta in range(n_red):
        other = lax.rem(mine + delta, n_red)
        ox, oc = other // n_occ, lax.rem(other, n_occ)
        if delta > 0:
            pl.semaphore_signal(barrier, inc=1, device_id={"aux": ox, "occ": oc}, device_id_type=MESH)
        for has, way in sides:
            @pl.when(has)
            def _():
                pl.semaphore_signal(
                    barrier, inc=1, device_id={"pair": z + way, "aux": ox, "occ": oc}, device_id_type=MESH)

    for move in small:
        move.wait()
    fun = lax.broadcasted_iota(jnp.int32, (width, orbitals), 0)
    masked = jnp.concatenate([
        jnp.where(fun < size[b], coef[b * width:(b + 1) * width, :].astype(jnp.float32), 0.0)
        for b in range(shells)], axis=0).astype(jnp.bfloat16)
    to = lax.broadcasted_iota(jnp.int32, (kept, functions), 0)
    frm = lax.broadcasted_iota(jnp.int32, (kept, functions), 1)
    g = lax.rem(frm, width)
    packing = jnp.logical_and(to == (frm // width) * top + g, g < top)
    narrow[...] = jnp.where(packing, 1.0, 0.0).astype(jnp.bfloat16)
    mine_cols = pl.ds(pl.multiple_of(c * orbitals, orbitals), orbitals)
    coefs[pl.ds(pl.multiple_of(z * kept, kept), kept), mine_cols] = jnp.dot(
        narrow[...], masked, preferred_element_type=jnp.float32).astype(jnp.bfloat16)
    to = lax.broadcasted_iota(jnp.int32, (functions, kept), 1)
    frm = lax.broadcasted_iota(jnp.int32, (functions, kept), 0)
    g = lax.rem(frm, width)
    packing = jnp.logical_and(to == (frm // width) * top + g, g < top)
    widen[...] = jnp.where(packing, 1.0, 0.0).astype(jnp.bfloat16)
    if nbas > n_pair * kept:
        coefs[n_pair * kept:, :] = jnp.zeros((nbas - n_pair * kept, n_occ * orbitals), jnp.bfloat16)

    row = lax.broadcasted_iota(jnp.int32, info.shape, 0)
    lane = lax.broadcasted_iota(jnp.int32, info.shape, 1)
    packed = jnp.zeros(info.shape, jnp.int32)
    for b in range(shells):
        line = jnp.where(lane == slots, cnt[b], jnp.where(lane == slots + 1, size[b], 0))
        for s in range(slots):
            line = jnp.where(lane == s, ket[b, s], line)
        packed = jnp.where(row == b, line, packed)
    info[...] = packed

    ups, downs = has_up.astype(jnp.int32), has_down.astype(jnp.int32)
    pl.semaphore_wait(barrier, n_red - 1 + n_red * (ups + downs))

    def part(owner, who):
        return coefs.at[pl.ds(pl.multiple_of(owner * kept, kept), kept),
                        pl.ds(pl.multiple_of(who * orbitals, orbitals), orbitals)]

    def hop(owner, way, s):
        k = 0 if way > 0 else 1
        return remote(lambda: part(owner, c), lambda: part(owner, c), lambda: coef_send.at[k, s],
                      lambda: coef_recv.at[k, s], pair=lambda: z + way)

    def across(owner, k, s, delta, who):
        return remote(lambda: part(owner, who), lambda: part(owner, who), lambda: coef_fwd.at[k, s, delta],
                      lambda: coef_cross.at[k, s, delta], occ=lambda: lax.rem(c + delta, n_occ))

    def across_in(owner, k, s, delta):
        return across(owner, k, s, delta, lax.rem(c - delta + n_occ, n_occ))

    def t_hop(k, j):
        way, side = (1, 1) if k == 0 else (-1, 0)
        return remote(lambda: t_pack.at[side, j], lambda: t_nb.at[side, j],
                      lambda: t_send.at[k, j], lambda: t_recv.at[side, j], pair=lambda: z + way)

    def info_hop(k):
        way = 1 if k == 0 else -1
        return remote(lambda: info, lambda: info_in.at[1 - k], lambda: info_send.at[k],
                      lambda: info_recv.at[1 - k], pair=lambda: z + way)

    def select(which, ket_at, cnt_at):
        col = lax.broadcasted_iota(jnp.int32, (width, nbas), 1) - lax.broadcasted_iota(jnp.int32, (width, nbas), 0)
        live = lax.broadcasted_iota(jnp.int32, (width, nbas), 0) < top

        @pl.loop(0, shells)
        def _(b):
            for s in range(slots):
                at = pl.multiple_of(b * span + s * width, width)
                hit = jnp.logical_and(jnp.logical_and(col == ket_at(b, s) * top, live), cnt_at(b) > s)
                pick[which, pl.ds(at, width), :] = jnp.where(hit, 1.0, 0.0).astype(jnp.bfloat16)

    def picked(which, b):
        return pick[which, pl.ds(pl.multiple_of(b * span, span), span), :]

    def scatter(which, lo, hi):
        @pl.loop(lo, hi)
        def _(b):
            spread[b] = jnp.dot(t_own[b], picked(which, b), preferred_element_type=jnp.float32).astype(jnp.bfloat16)

    for k, (has, way) in enumerate(sides):
        begin(hop(z, way, 0), has)
    for delta in range(1, n_occ):
        begin(across(z, 0, n_pair - 1, delta, c))
    for k, (has, way) in enumerate(sides):
        begin(info_hop(k), has)
    select(2, lambda b, s: ket[b, s], lambda b: cnt[b])
    local.wait()

    for side in range(2):
        for j in range(chunks):
            at = side * half_rows + j * step
            packed = jnp.dot(narrow[...], jnp.concatenate([t_own[b, at:at + step, :] for b in range(shells)], axis=1),
                             preferred_element_type=jnp.float32).astype(jnp.bfloat16)
            for b in range(shells):
                t_pack[side, j, b] = packed[:, b * span:(b + 1) * span]

    for s in range(n_pair - 1):
        for k, (has, way) in enumerate(sides):
            owner = z - way * (s + 1)
            here = (owner >= 0) if way > 0 else (owner < n_pair)
            arrive(hop(owner, way, s), here)
            if s < n_pair - 2:
                begin(hop(owner, way, s + 1), jnp.logical_and(here, has))
            for delta in range(1, n_occ):
                begin(across(owner, k, s, delta, c), here)
        if s == max(n_pair - 3, 0):
            for j in range(chunks):
                for k, (has, way) in enumerate(sides):
                    begin(t_hop(k, j), has)
        if s == 0:
            scatter(2, 0, shells // 2)
        if s == 1 or n_pair == 2:
            scatter(2, shells // 2, shells)
    for delta in range(1, n_occ):
        arrive(across_in(z, 0, n_pair - 1, delta))
    for s in range(n_pair - 1):
        for k, (has, way) in enumerate(sides):
            owner = z - way * (s + 1)
            here = (owner >= 0) if way > 0 else (owner < n_pair)
            for delta in range(1, n_occ):
                arrive(across_in(owner, k, s, delta), here)

    lines = 384 if nbas % 384 == 0 else 128

    @pl.loop(0, nbas // lines)
    def _(i):
        at = pl.ds(pl.multiple_of(i * lines, lines), lines)
        d = lax.dot_general(coefs[at, :], coefs[...], NT, preferred_element_type=jnp.float32)
        high = d.astype(jnp.bfloat16)
        density[at, :nbas] = high
        density[at, nbas:] = (d - high.astype(jnp.float32)).astype(jnp.bfloat16)

    together = 4

    @pl.loop(0, shells // together)
    def _(i):
        at = pl.multiple_of(i * together * span, together * span)
        w = jnp.dot(pick[2, pl.ds(at, together * span), :], density[...],
                    preferred_element_type=jnp.float32).astype(jnp.bfloat16)
        w = w.reshape(together, span, 2 * nbas)
        weights[pl.ds(i * together, together), :span, :] = w[:, :, :nbas]
        weights[pl.ds(i * together, together), span:, :] = w[:, :, nbas:]

    @pl.loop(0, shells, unroll=2)
    def _(b):
        t = t_own[b]
        left[b] = jnp.dot(jnp.concatenate([t, t], axis=1), weights[b],
                          preferred_element_type=jnp.float32).astype(jnp.bfloat16)

    tiles[...] = jnp.zeros_like(tiles)
    unroll = 8

    def pages(ref, at):
        return jnp.concatenate([
            ref[:, pl.ds(pl.multiple_of(at + u * width, width), width), :].reshape(functions, nbas)
            for u in range(unroll)], axis=1)

    def contract(other, at, count, off, col):
        def body(i, acc):
            p = i * unroll * width
            return acc + lax.dot_general(pages(left, at + p), pages(other, p + off), NT,
                                         preferred_element_type=jnp.float32)
        zero = jnp.zeros((functions, functions), jnp.float32)
        tiles[:, col:col + functions] += lax.fori_loop(0, count // width // unroll, body, zero)

    contract(spread, 0, rows, 0, functions)
    for side, (has, way) in enumerate(sides):
        @pl.when(has)
        def _():
            info_hop(1 - side)().wait_recv()
            move = pltpu.make_async_copy(info_in.at[side], info_s.at[side], local_sem.at[1 + side])
            move.start()
            move.wait()
            select(side, lambda b, s: info_s[side, b, s], lambda b: info_s[side, b, slots])
    for j in range(chunks):
        for side, (has, way) in enumerate(sides):
            @pl.when(has)
            def _():
                t_hop(1 - side, j)().wait_recv()
                at = side * half_rows + j * step

                blocks = jnp.dot(widen[...], jnp.concatenate([t_nb[side, j, b] for b in range(shells)], axis=1),
                                 preferred_element_type=jnp.float32).astype(jnp.bfloat16)
                for b in range(shells):
                    spread_nb[b] = jnp.dot(blocks[:, b * span:(b + 1) * span], pick[side, b * span:(b + 1) * span, :],
                                           preferred_element_type=jnp.float32).astype(jnp.bfloat16)
                contract(spread_nb, at, step, 0, 2 * functions if side == 0 else 0)
    flips[0] = tiles[:, 2 * functions:].T
    flips[1] = tiles[:, :functions].T

    def cut(ref, r):
        return ref.at[pl.ds(pl.multiple_of(r * out_rows, out_rows), out_rows), :]

    def same(delta):
        other = lax.rem(mine + delta, n_red)
        return remote(lambda: cut(tiles, other), lambda: red_same.at[delta], lambda: same_send.at[delta],
                      lambda: same_recv.at[delta], aux=lambda: other // n_occ, occ=lambda: lax.rem(other, n_occ))

    def cross(side, delta):
        other = lax.rem(mine + delta, n_red)
        way = 1 if side == 0 else -1
        return remote(lambda: cut(flips.at[side], other), lambda: red_cross.at[side, delta],
                      lambda: cross_send.at[side, delta], lambda: cross_recv.at[side, delta],
                      pair=lambda: z + way, aux=lambda: other // n_occ, occ=lambda: lax.rem(other, n_occ))

    for delta in range(n_red):
        for side, (has, way) in enumerate(sides):
            begin(cross(side, delta), has)
    for delta in range(1, n_red):
        begin(same(delta))

    total = tiles[pl.ds(pl.multiple_of(mine * out_rows, out_rows), out_rows), :]
    for delta in range(1, n_red):
        arrive(same(delta))
        total = total + red_same[delta]
    tiles_out = [total[:, i * functions:(i + 1) * functions] for i in range(3)]
    for side, (has, way) in enumerate(sides):
        comes = has_down if side == 0 else has_up
        for delta in range(n_red):
            arrive(cross(side, delta), comes)
        col = 0 if side == 0 else 2
        more = red_cross[side, 0]
        for delta in range(1, n_red):
            more = more + red_cross[side, delta]
        tiles_out[col] = jnp.where(comes, tiles_out[col] + more, 0.0)

    scale = 1.0 / math.sqrt(rows // width * n_red * orbitals * n_occ)
    r_id = lax.broadcasted_iota(jnp.int32, (out_rows, functions), 0) + mine * out_rows
    c_id = lax.broadcasted_iota(jnp.int32, (out_rows, functions), 1)
    r_size = jnp.zeros_like(r_id)
    for b in range(shells):
        r_size = jnp.where(r_id // width == b, size[b], r_size)
    r_live = lax.rem(r_id, width) < r_size
    for i in range(3):
        c_size = jnp.zeros_like(c_id)
        for b in range(shells):
            there = size[b] if i == 1 else info_s[1 if i == 0 else 0, b, slots + 1]
            c_size = jnp.where(c_id // width == b, there, c_size)
        live = jnp.logical_and(r_live, lax.rem(c_id, width) < c_size)
        out[:, i * functions:(i + 1) * functions] = jnp.where(live, tiles_out[i] * scale, 0.0)

    for cond, make in pending:
        when(cond, make, lambda d: d.wait_send())


def shards(three_index, coefficients, shell_size, ket_shell, ket_count):
    shells, aux_rows, width, span = three_index.shape
    slots = span // width
    n_pair, n_aux, n_occ = (lax.axis_size(a) for a in ("pair", "aux", "occ"))
    n_red = n_aux * n_occ
    orbitals = coefficients.shape[1]
    functions = shells * width
    rows = aux_rows * width // n_occ
    thin = shells * (width * 5 // 8)
    nbas = -(-n_pair * thin // 128) * 128
    chunks = rows // 2 // functions
    out_rows = functions // n_red
    step = functions
    bf16, f32 = jnp.bfloat16, jnp.float32
    dma = pltpu.SemaphoreType.DMA
    vmem = pl.BlockSpec(memory_space=pltpu.VMEM)
    return pl.pallas_call(
        functools.partial(kernel, (n_pair, n_aux, n_occ, width, slots, chunks)),
        out_shape=jax.ShapeDtypeStruct((out_rows, 3 * functions), f32),
        in_specs=[pl.BlockSpec(memory_space=pl.ANY)] * 5,
        out_specs=vmem,
        scratch_shapes=[
            pltpu.VMEM((functions, orbitals), bf16),
            pltpu.SMEM((shells,), jnp.int32),
            pltpu.SMEM((shells, slots), jnp.int32),
            pltpu.SMEM((shells,), jnp.int32),
            pltpu.VMEM((shells, rows, span), bf16),
            pltpu.VMEM((2, chunks, shells, thin, span), bf16),
            pltpu.VMEM((nbas, n_occ * orbitals), bf16),
            pltpu.VMEM((3, shells * span, nbas), bf16),
            pltpu.VMEM((thin, functions), bf16),
            pltpu.VMEM((functions, thin), bf16),
            pltpu.VMEM((2, chunks, shells, thin, span), bf16),
            pltpu.VMEM((nbas, 2 * nbas), bf16),
            pltpu.VMEM((shells, 2 * span, nbas), bf16),
            pltpu.VMEM((shells, rows, nbas), bf16),
            pltpu.VMEM((shells, rows, nbas), bf16),
            pltpu.VMEM((shells, step, nbas), bf16),
            pltpu.VMEM((shells, 128), jnp.int32),
            pltpu.VMEM((2, shells, 128), jnp.int32),
            pltpu.SMEM((2, shells, 128), jnp.int32),
            pltpu.VMEM((functions, 3 * functions), f32),
            pltpu.VMEM((2, functions, functions), f32),
            pltpu.VMEM((n_red, out_rows, 3 * functions), f32),
            pltpu.VMEM((2, n_red, out_rows, functions), f32),
            dma((7,)),
            dma((2, n_pair)),
            dma((2, n_pair)),
            dma((2, n_pair, n_occ)),
            dma((2, n_pair, n_occ)),
            dma((2,)),
            dma((2,)),
            dma((2, chunks)),
            dma((2, chunks)),
            dma((n_red,)),
            dma((n_red,)),
            dma((2, n_red)),
            dma((2, n_red)),
        ],
        compiler_params=pltpu.CompilerParams(
            collective_id=0, has_side_effects=True, vmem_limit_bytes=64 * 1024 * 1024),
    )(three_index.reshape(shells, aux_rows * width, span), coefficients, shell_size, ket_shell, ket_count)


def solution(mesh):
    return jax.shard_map(
        shards,
        mesh=mesh,
        in_specs=(
            P(("parts", "pair"), "aux", None, None),
            P(("parts", "pair"), "occ"),
            P(("parts", "pair")),
            P(("parts", "pair"), None),
            P(("parts", "pair")),
        ),
        out_specs=P(("parts", "pair", "aux", "occ"), None),
        check_vma=False,
    )
```

```python
import functools
import math

import jax
import jax.numpy as jnp
from jax import lax
from jax.experimental import pallas as pl
from jax.experimental.pallas import tpu as pltpu
from jax.sharding import PartitionSpec as P

MESH = pl.DeviceIdType.MESH
NT = (((1,), (1,)), ((), ()))


def kernel(sizes, t_hbm, coef_hbm, size_hbm, ket_hbm, cnt_hbm, out, coef, size, ket, cnt, t_own, t_nb, coefs, pick, narrow, widen, t_pack, density, weights, left, spread, spread_nb, info,
           info_in, info_s, tiles, flips, red_same, red_cross, local_sem, coef_send, coef_recv, coef_fwd, coef_cross,
           info_send, info_recv, t_send, t_recv, same_send, same_recv, cross_send, cross_recv):
    n_pair, n_aux, n_occ, width, slots, chunks = sizes
    shells, rows, span = t_own.shape
    orbitals = coef.shape[1]
    functions = shells * width
    n_red = n_aux * n_occ
    half_rows = rows // 2
    step = half_rows // chunks
    out_rows = functions // n_red
    top = width * 5 // 8
    kept = shells * top
    nbas = coefs.shape[0]
    z = lax.axis_index("pair")
    x = lax.axis_index("aux")
    c = lax.axis_index("occ")
    mine = x * n_occ + c
    base = pl.multiple_of(c * rows, rows)
    has_up = z + 1 < n_pair
    has_down = z > 0
    sides = ((has_up, 1), (has_down, -1))
    pending = []

    def when(cond, make, act):
        if cond is None:
            act(make())
        else:
            @pl.when(cond)
            def _():
                act(make())

    def begin(make, cond=None):
        when(cond, make, lambda d: d.start())
        pending.append((cond, make))

    def arrive(make, cond=None):
        when(cond, make, lambda d: d.wait_recv())

    def remote(src, dst, s_sem, r_sem, **where):
        return lambda: pltpu.make_async_remote_copy(
            src_ref=src(), dst_ref=dst(), send_sem=s_sem(), recv_sem=r_sem(),
            device_id={k: v() for k, v in where.items()}, device_id_type=MESH)

    local = pltpu.make_async_copy(t_hbm.at[:, pl.ds(base, rows), :], t_own, local_sem.at[0])
    small = [pltpu.make_async_copy(src, dst, local_sem.at[3 + i]) for i, (src, dst) in enumerate(
        ((size_hbm, size), (coef_hbm, coef), (ket_hbm, ket), (cnt_hbm, cnt)))]
    for move in small:
        move.start()
    local.start()

    barrier = pltpu.get_barrier_semaphore()
    for delta in range(n_red):
        other = lax.rem(mine + delta, n_red)
        ox, oc = other // n_occ, lax.rem(other, n_occ)
        if delta > 0:
            pl.semaphore_signal(barrier, inc=1, device_id={"aux": ox, "occ": oc}, device_id_type=MESH)
        for has, way in sides:
            @pl.when(has)
            def _():
                pl.semaphore_signal(
                    barrier, inc=1, device_id={"pair": z + way, "aux": ox, "occ": oc}, device_id_type=MESH)

    for move in small:
        move.wait()
    fun = lax.broadcasted_iota(jnp.int32, (width, orbitals), 0)
    masked = jnp.concatenate([
        jnp.where(fun < size[b], coef[b * width:(b + 1) * width, :].astype(jnp.float32), 0.0)
        for b in range(shells)], axis=0).astype(jnp.bfloat16)
    to = lax.broadcasted_iota(jnp.int32, (kept, functions), 0)
    frm = lax.broadcasted_iota(jnp.int32, (kept, functions), 1)
    g = lax.rem(frm, width)
    packing = jnp.logical_and(to == (frm // width) * top + g, g < top)
    narrow[...] = jnp.where(packing, 1.0, 0.0).astype(jnp.bfloat16)
    mine_cols = pl.ds(pl.multiple_of(c * orbitals, orbitals), orbitals)
    coefs[pl.ds(pl.multiple_of(z * kept, kept), kept), mine_cols] = jnp.dot(
        narrow[...], masked, preferred_element_type=jnp.float32).astype(jnp.bfloat16)
    to = lax.broadcasted_iota(jnp.int32, (functions, kept), 1)
    frm = lax.broadcasted_iota(jnp.int32, (functions, kept), 0)
    g = lax.rem(frm, width)
    packing = jnp.logical_and(to == (frm // width) * top + g, g < top)
    widen[...] = jnp.where(packing, 1.0, 0.0).astype(jnp.bfloat16)
    if nbas > n_pair * kept:
        coefs[n_pair * kept:, :] = jnp.zeros((nbas - n_pair * kept, n_occ * orbitals), jnp.bfloat16)

    row = lax.broadcasted_iota(jnp.int32, info.shape, 0)
    lane = lax.broadcasted_iota(jnp.int32, info.shape, 1)
    packed = jnp.zeros(info.shape, jnp.int32)
    for b in range(shells):
        line = jnp.where(lane == slots, cnt[b], jnp.where(lane == slots + 1, size[b], 0))
        for s in range(slots):
            line = jnp.where(lane == s, ket[b, s], line)
        packed = jnp.where(row == b, line, packed)
    info[...] = packed

    ups, downs = has_up.astype(jnp.int32), has_down.astype(jnp.int32)
    pl.semaphore_wait(barrier, n_red - 1 + n_red * (ups + downs))

    def part(owner, who):
        return coefs.at[pl.ds(pl.multiple_of(owner * kept, kept), kept),
                        pl.ds(pl.multiple_of(who * orbitals, orbitals), orbitals)]

    def hop(owner, way, s):
        k = 0 if way > 0 else 1
        return remote(lambda: part(owner, c), lambda: part(owner, c), lambda: coef_send.at[k, s],
                      lambda: coef_recv.at[k, s], pair=lambda: z + way)

    def across(owner, k, s, delta, who):
        return remote(lambda: part(owner, who), lambda: part(owner, who), lambda: coef_fwd.at[k, s, delta],
                      lambda: coef_cross.at[k, s, delta], occ=lambda: lax.rem(c + delta, n_occ))

    def across_in(owner, k, s, delta):
        return across(owner, k, s, delta, lax.rem(c - delta + n_occ, n_occ))

    def t_hop(k, j):
        way, side = (1, 1) if k == 0 else (-1, 0)
        return remote(lambda: t_pack.at[side, j], lambda: t_nb.at[side, j],
                      lambda: t_send.at[k, j], lambda: t_recv.at[side, j], pair=lambda: z + way)

    def info_hop(k):
        way = 1 if k == 0 else -1
        return remote(lambda: info, lambda: info_in.at[1 - k], lambda: info_send.at[k],
                      lambda: info_recv.at[1 - k], pair=lambda: z + way)

    def select(which, ket_at, cnt_at):
        col = lax.broadcasted_iota(jnp.int32, (width, nbas), 1) - lax.broadcasted_iota(jnp.int32, (width, nbas), 0)
        live = lax.broadcasted_iota(jnp.int32, (width, nbas), 0) < top

        @pl.loop(0, shells)
        def _(b):
            for s in range(slots):
                at = pl.multiple_of(b * span + s * width, width)
                hit = jnp.logical_and(jnp.logical_and(col == ket_at(b, s) * top, live), cnt_at(b) > s)
                pick[which, pl.ds(at, width), :] = jnp.where(hit, 1.0, 0.0).astype(jnp.bfloat16)

    def picked(which, b):
        return pick[which, pl.ds(pl.multiple_of(b * span, span), span), :]

    def scatter(which, lo, hi):
        @pl.loop(lo, hi)
        def _(b):
            spread[b] = jnp.dot(t_own[b], picked(which, b), preferred_element_type=jnp.float32).astype(jnp.bfloat16)

    for k, (has, way) in enumerate(sides):
        begin(hop(z, way, 0), has)
    for delta in range(1, n_occ):
        begin(across(z, 0, n_pair - 1, delta, c))
    for k, (has, way) in enumerate(sides):
        begin(info_hop(k), has)
    select(2, lambda b, s: ket[b, s], lambda b: cnt[b])
    local.wait()

    for side in range(2):
        for j in range(chunks):
            at = side * half_rows + j * step
            packed = jnp.dot(narrow[...], jnp.concatenate([t_own[b, at:at + step, :] for b in range(shells)], axis=1),
                             preferred_element_type=jnp.float32).astype(jnp.bfloat16)
            for b in range(shells):
                t_pack[side, j, b] = packed[:, b * span:(b + 1) * span]

    for s in range(n_pair - 1):
        for k, (has, way) in enumerate(sides):
            owner = z - way * (s + 1)
            here = (owner >= 0) if way > 0 else (owner < n_pair)
            arrive(hop(owner, way, s), here)
            if s < n_pair - 2:
                begin(hop(owner, way, s + 1), jnp.logical_and(here, has))
            for delta in range(1, n_occ):
                begin(across(owner, k, s, delta, c), here)
        if s == max(n_pair - 3, 0):
            for j in range(chunks):
                for k, (has, way) in enumerate(sides):
                    begin(t_hop(k, j), has)
        if s == 0:
            scatter(2, 0, shells // 2)
        if s == 1 or n_pair == 2:
            scatter(2, shells // 2, shells)
            for side, (has, way) in enumerate(sides):
                @pl.when(has)
                def _():
                    info_hop(1 - side)().wait_recv()
                    move = pltpu.make_async_copy(info_in.at[side], info_s.at[side], local_sem.at[1 + side])
                    move.start()
                    move.wait()
                    select(side, lambda b, s: info_s[side, b, s], lambda b: info_s[side, b, slots])
    for delta in range(1, n_occ):
        arrive(across_in(z, 0, n_pair - 1, delta))
    for s in range(n_pair - 1):
        for k, (has, way) in enumerate(sides):
            owner = z - way * (s + 1)
            here = (owner >= 0) if way > 0 else (owner < n_pair)
            for delta in range(1, n_occ):
                arrive(across_in(owner, k, s, delta), here)

    lines = 384 if nbas % 384 == 0 else 128

    @pl.loop(0, nbas // lines)
    def _(i):
        at = pl.ds(pl.multiple_of(i * lines, lines), lines)
        d = lax.dot_general(coefs[at, :], coefs[...], NT, preferred_element_type=jnp.float32)
        high = d.astype(jnp.bfloat16)
        density[at, :nbas] = high
        density[at, nbas:] = (d - high.astype(jnp.float32)).astype(jnp.bfloat16)

    together = 4

    @pl.loop(0, shells // together)
    def _(i):
        at = pl.multiple_of(i * together * span, together * span)
        w = jnp.dot(pick[2, pl.ds(at, together * span), :], density[...],
                    preferred_element_type=jnp.float32).astype(jnp.bfloat16)
        w = w.reshape(together, span, 2 * nbas)
        weights[pl.ds(i * together, together), :span, :] = w[:, :, :nbas]
        weights[pl.ds(i * together, together), span:, :] = w[:, :, nbas:]

    @pl.loop(0, shells, unroll=2)
    def _(b):
        t = t_own[b]
        left[b] = jnp.dot(jnp.concatenate([t, t], axis=1), weights[b],
                          preferred_element_type=jnp.float32).astype(jnp.bfloat16)

    tiles[...] = jnp.zeros_like(tiles)
    unroll = 8

    def pages(ref, at):
        return jnp.concatenate([
            ref[:, pl.ds(pl.multiple_of(at + u * width, width), width), :].reshape(functions, nbas)
            for u in range(unroll)], axis=1)

    def contract(other, at, count, off, col):
        def body(i, acc):
            p = i * unroll * width
            return acc + lax.dot_general(pages(left, at + p), pages(other, p + off), NT,
                                         preferred_element_type=jnp.float32)
        zero = jnp.zeros((functions, functions), jnp.float32)
        tiles[:, col:col + functions] += lax.fori_loop(0, count // width // unroll, body, zero)

    contract(spread, 0, rows, 0, functions)
    for j in range(chunks):
        for side, (has, way) in enumerate(sides):
            @pl.when(has)
            def _():
                t_hop(1 - side, j)().wait_recv()
                at = side * half_rows + j * step

                blocks = jnp.dot(widen[...], jnp.concatenate([t_nb[side, j, b] for b in range(shells)], axis=1),
                                 preferred_element_type=jnp.float32).astype(jnp.bfloat16)
                for b in range(shells):
                    spread_nb[b] = jnp.dot(blocks[:, b * span:(b + 1) * span], pick[side, b * span:(b + 1) * span, :],
                                           preferred_element_type=jnp.float32).astype(jnp.bfloat16)
                contract(spread_nb, at, step, 0, 2 * functions if side == 0 else 0)
    flips[0] = tiles[:, 2 * functions:].T
    flips[1] = tiles[:, :functions].T

    def cut(ref, r):
        return ref.at[pl.ds(pl.multiple_of(r * out_rows, out_rows), out_rows), :]

    def same(delta):
        other = lax.rem(mine + delta, n_red)
        return remote(lambda: cut(tiles, other), lambda: red_same.at[delta], lambda: same_send.at[delta],
                      lambda: same_recv.at[delta], aux=lambda: other // n_occ, occ=lambda: lax.rem(other, n_occ))

    def cross(side, delta):
        other = lax.rem(mine + delta, n_red)
        way = 1 if side == 0 else -1
        return remote(lambda: cut(flips.at[side], other), lambda: red_cross.at[side, delta],
                      lambda: cross_send.at[side, delta], lambda: cross_recv.at[side, delta],
                      pair=lambda: z + way, aux=lambda: other // n_occ, occ=lambda: lax.rem(other, n_occ))

    for delta in range(n_red):
        for side, (has, way) in enumerate(sides):
            begin(cross(side, delta), has)
    for delta in range(1, n_red):
        begin(same(delta))

    total = tiles[pl.ds(pl.multiple_of(mine * out_rows, out_rows), out_rows), :]
    for delta in range(1, n_red):
        arrive(same(delta))
        total = total + red_same[delta]
    tiles_out = [total[:, i * functions:(i + 1) * functions] for i in range(3)]
    for side, (has, way) in enumerate(sides):
        comes = has_down if side == 0 else has_up
        for delta in range(n_red):
            arrive(cross(side, delta), comes)
        col = 0 if side == 0 else 2
        more = red_cross[side, 0]
        for delta in range(1, n_red):
            more = more + red_cross[side, delta]
        tiles_out[col] = jnp.where(comes, tiles_out[col] + more, 0.0)

    scale = 1.0 / math.sqrt(rows // width * n_red * orbitals * n_occ)
    r_id = lax.broadcasted_iota(jnp.int32, (out_rows, functions), 0) + mine * out_rows
    c_id = lax.broadcasted_iota(jnp.int32, (out_rows, functions), 1)
    r_size = jnp.zeros_like(r_id)
    for b in range(shells):
        r_size = jnp.where(r_id // width == b, size[b], r_size)
    r_live = lax.rem(r_id, width) < r_size
    for i in range(3):
        c_size = jnp.zeros_like(c_id)
        for b in range(shells):
            there = size[b] if i == 1 else info_s[1 if i == 0 else 0, b, slots + 1]
            c_size = jnp.where(c_id // width == b, there, c_size)
        live = jnp.logical_and(r_live, lax.rem(c_id, width) < c_size)
        out[:, i * functions:(i + 1) * functions] = jnp.where(live, tiles_out[i] * scale, 0.0)

    for cond, make in pending:
        when(cond, make, lambda d: d.wait_send())


def shards(three_index, coefficients, shell_size, ket_shell, ket_count):
    shells, aux_rows, width, span = three_index.shape
    slots = span // width
    n_pair, n_aux, n_occ = (lax.axis_size(a) for a in ("pair", "aux", "occ"))
    n_red = n_aux * n_occ
    orbitals = coefficients.shape[1]
    functions = shells * width
    rows = aux_rows * width // n_occ
    thin = shells * (width * 5 // 8)
    nbas = -(-n_pair * thin // 128) * 128
    chunks = rows // 2 // functions
    out_rows = functions // n_red
    step = functions
    bf16, f32 = jnp.bfloat16, jnp.float32
    dma = pltpu.SemaphoreType.DMA
    vmem = pl.BlockSpec(memory_space=pltpu.VMEM)
    return pl.pallas_call(
        functools.partial(kernel, (n_pair, n_aux, n_occ, width, slots, chunks)),
        out_shape=jax.ShapeDtypeStruct((out_rows, 3 * functions), f32),
        in_specs=[pl.BlockSpec(memory_space=pl.ANY)] * 5,
        out_specs=vmem,
        scratch_shapes=[
            pltpu.VMEM((functions, orbitals), bf16),
            pltpu.SMEM((shells,), jnp.int32),
            pltpu.SMEM((shells, slots), jnp.int32),
            pltpu.SMEM((shells,), jnp.int32),
            pltpu.VMEM((shells, rows, span), bf16),
            pltpu.VMEM((2, chunks, shells, thin, span), bf16),
            pltpu.VMEM((nbas, n_occ * orbitals), bf16),
            pltpu.VMEM((3, shells * span, nbas), bf16),
            pltpu.VMEM((thin, functions), bf16),
            pltpu.VMEM((functions, thin), bf16),
            pltpu.VMEM((2, chunks, shells, thin, span), bf16),
            pltpu.VMEM((nbas, 2 * nbas), bf16),
            pltpu.VMEM((shells, 2 * span, nbas), bf16),
            pltpu.VMEM((shells, rows, nbas), bf16),
            pltpu.VMEM((shells, rows, nbas), bf16),
            pltpu.VMEM((shells, step, nbas), bf16),
            pltpu.VMEM((shells, 128), jnp.int32),
            pltpu.VMEM((2, shells, 128), jnp.int32),
            pltpu.SMEM((2, shells, 128), jnp.int32),
            pltpu.VMEM((functions, 3 * functions), f32),
            pltpu.VMEM((2, functions, functions), f32),
            pltpu.VMEM((n_red, out_rows, 3 * functions), f32),
            pltpu.VMEM((2, n_red, out_rows, functions), f32),
            dma((7,)),
            dma((2, n_pair)),
            dma((2, n_pair)),
            dma((2, n_pair, n_occ)),
            dma((2, n_pair, n_occ)),
            dma((2,)),
            dma((2,)),
            dma((2, chunks)),
            dma((2, chunks)),
            dma((n_red,)),
            dma((n_red,)),
            dma((2, n_red)),
            dma((2, n_red)),
        ],
        compiler_params=pltpu.CompilerParams(
            collective_id=0, has_side_effects=True, vmem_limit_bytes=64 * 1024 * 1024),
    )(three_index.reshape(shells, aux_rows * width, span), coefficients, shell_size, ket_shell, ket_count)


def solution(mesh):
    return jax.shard_map(
        shards,
        mesh=mesh,
        in_specs=(
            P(("parts", "pair"), "aux", None, None),
            P(("parts", "pair"), "occ"),
            P(("parts", "pair")),
            P(("parts", "pair"), None),
            P(("parts", "pair")),
        ),
        out_specs=P(("parts", "pair", "aux", "occ"), None),
        check_vma=False,
    )
```
